32 devices in a mesh: frame: 32 (over z, y, x, core).
Axes of the slice: x: 2, y: 2, z: 4, core: 2. Of those that a mesh axis runs over, the one named last changes fastest.
Arguments:
- tokens: bfloat16 [49152, 128], P('frame'), may hold values from -8 to 8
- fine_map: bfloat16 [1536, 128, 128], P('frame'), may hold values from -8 to 8
- matches: int32 [32, 2, 2, 512], P('frame'), may hold values from 0 to 1535
- subcells: int32 [32, 2, 2, 512], P('frame'), may hold values from 0 to 3
- counts: int32 [32, 2], P('frame'), may hold values from 64 to 512, as said below
Outputs:
- confidence: float32 [32, 2, 512], P('frame')
- offsets: float32 [32, 2, 2, 512], P('frame')
The draws below stay inside these ranges and needn't reach their ends.
Inputs may be any that keep to these rules, and one draw needn't show every extreme that they name: `counts`: for each round some frame has exactly 512 valid slots; slots at or beyond the count are ignored.
All inputs are finite; a program needn't handle non-finite values.
Results may differ from the reference program's by a relative error of at most 0.0003.
Values may be sent and summed in bfloat16 or wider, within the bound.
No kernel may reach another device: no remote copies, remote signals or barrier semaphores. Data moves between devices by JAX's collectives and lax.ppermute only.
A program may use at most 64 MiB of HBM per device.

```python
import math
import jax
import jax.numpy as jnp
import numpy as np
from jax import lax

C = 128
CF = 128
WC = 64
M = 512
ROUNDS = 2
TOK = 1536
FH = 48
FW = 128
FRAMES = 32


def draw_tokens(key, part):
    key_base = jax.random.fold_in(jax.random.fold_in(key, 11), 0)
    rows = FRAMES * TOK
    values = jnp.clip(jax.random.normal(key_base, (rows, C), jnp.float32), -4.0, 4.0)
    return values.astype(jnp.bfloat16)


def draw_fine_map(key, part):
    key_base = jax.random.fold_in(jax.random.fold_in(key, 23), 0)
    rows = FRAMES * FH
    values = jnp.clip(jax.random.normal(key_base, (rows, FW, CF), jnp.float32), -4.0, 4.0)
    return values.astype(jnp.bfloat16)


def draw_counts(key, part):
    key_low, key_high, key_pick, key_full = jax.random.split(jax.random.fold_in(key, 37), 4)
    base = jax.random.randint(key_low, (FRAMES, ROUNDS), M // 8, M // 2 + 1)
    heavy = jax.random.randint(key_high, (FRAMES, ROUNDS), M // 2, M + 1)
    picked = jax.random.randint(key_pick, (FRAMES, ROUNDS), 0, 8) == 0
    amount = jnp.where(picked, heavy, base)
    fullest = jax.random.randint(key_full, (ROUNDS,), 0, FRAMES)
    amount = jnp.where(jnp.arange(FRAMES, dtype=jnp.int32)[:, None] == fullest[None, :], M, amount)
    return amount.astype(jnp.int32)


def touch_ends(drawn, own_key, low, top_value):
    place = [jax.random.randint(jax.random.fold_in(own_key, axis), (), 0, length) for axis, length in enumerate(drawn.shape)]
    main_axis = drawn.shape.index(max(drawn.shape))
    beside = place[:main_axis] + [(place[main_axis] + 1) % drawn.shape[main_axis]] + place[main_axis + 1:]
    return drawn.at[tuple(place)].set(low).at[tuple(beside)].set(top_value)


def setup_inputs(seed: int = 0) -> dict:
    seeds = jax.random.split(jax.random.key(seed), 6)
    tokens = draw_tokens(jax.random.fold_in(seeds[5], 71), 0)
    fine_map = draw_fine_map(jax.random.fold_in(seeds[5], 71), 0)
    matches = touch_ends(jax.random.randint(seeds[2], (FRAMES, ROUNDS, 2, M), 0, TOK), jax.random.fold_in(seeds[2], 1), 0, TOK - 1).astype(jnp.int32)
    subcells = touch_ends(jax.random.randint(seeds[3], (FRAMES, ROUNDS, 2, M), 0, 4), jax.random.fold_in(seeds[3], 1), 0, 3).astype(jnp.int32)
    counts = draw_counts(jax.random.fold_in(seeds[5], 71), 0)
    return {"tokens": tokens, "fine_map": fine_map, "matches": matches, "subcells": subcells, "counts": counts}


def crop_tiles(flat_map, cells, subs):
    cell_y = 2 * (cells // WC) + subs // 2
    cell_x = 2 * (cells % WC) + subs % 2
    spots = jnp.arange(25, dtype=jnp.int32)
    delta_y = spots // 5 - 2
    delta_x = spots % 5 - 2
    near_y = cell_y[:, None] + delta_y[None, :]
    near_x = cell_x[:, None] + delta_x[None, :]
    inside = (near_y >= 0) & (near_y < FH) & (near_x >= 0) & (near_x < FW)
    index = jnp.clip(near_y, 0, FH - 1) * FW + jnp.clip(near_x, 0, FW - 1)
    return flat_map[index] * inside[:, :, None].astype(flat_map.dtype)


def fine_offsets(tiles, query):
    heat = jnp.einsum("mjc,mc->mj", tiles.astype(jnp.float32), query.astype(jnp.float32)) * (CF ** -0.5)
    heat = heat - jnp.max(heat, axis=1, keepdims=True)
    expo = jnp.exp(heat)
    weight = expo / jnp.sum(expo, axis=1, keepdims=True)
    spots = jnp.arange(25, dtype=jnp.int32)
    delta_y = (spots // 5 - 2).astype(jnp.float32)
    delta_x = (spots % 5 - 2).astype(jnp.float32)
    return jnp.stack([jnp.sum(weight * delta_x[None, :], axis=1), jnp.sum(weight * delta_y[None, :], axis=1)])


def reference(tokens, fine_map, matches, subcells, counts):
    scale = 10.0 / C
    frame_tok = tokens.reshape(FRAMES, TOK, C)
    maps = fine_map.reshape(FRAMES, FH * FW, CF)
    conf_rounds = []
    offset_rounds = []
    for rnd in range(ROUNDS):
        bit = FRAMES >> (rnd + 1)
        ids = np.arange(FRAMES)
        lows = ids[(ids & bit) == 0]

        def pair_stats(low):
            scores = jnp.dot(frame_tok[low], frame_tok[low + bit].T, preferred_element_type=jnp.float32) * scale
            return jax.nn.logsumexp(scores, axis=1), jax.nn.logsumexp(scores, axis=0)

        row_lse, col_lse = lax.map(pair_stats, jnp.asarray(lows, dtype=jnp.int32))
        lse = jnp.zeros((FRAMES, TOK), jnp.float32).at[lows].set(row_lse).at[lows + bit].set(col_lse)

        def frame_out(frame):
            other = jnp.bitwise_xor(frame, jnp.int32(bit)).astype(jnp.int32)
            own_cells = matches[frame, rnd, 0]
            far_cells = matches[frame, rnd, 1]
            own_rows = frame_tok[frame][own_cells].astype(jnp.float32)
            far_rows = frame_tok[other][far_cells].astype(jnp.float32)
            score = jnp.sum(own_rows * far_rows, axis=1) * scale
            conf = 2.0 * score - lse[frame][own_cells] - lse[other][far_cells] + 2.0 * math.log(TOK)
            valid = jnp.arange(M, dtype=jnp.int32) < counts[frame, rnd]
            own_sub = subcells[frame, rnd, 0]
            cell_y = 2 * (own_cells // WC) + own_sub // 2
            cell_x = 2 * (own_cells % WC) + own_sub % 2
            query = maps[frame][cell_y * FW + cell_x]
            tiles = crop_tiles(maps[other], far_cells, subcells[frame, rnd, 1])
            offs = fine_offsets(tiles, query)
            return jnp.where(valid, conf, 0.0), jnp.where(valid[None, :], offs, 0.0)

        conf, offs = lax.map(frame_out, jnp.arange(FRAMES, dtype=jnp.int32))
        conf_rounds.append(conf)
        offset_rounds.append(offs)
    return jnp.stack(conf_rounds, axis=1), jnp.stack(offset_rounds, axis=1)
```

```python
import functools
import math

import jax
import jax.numpy as jnp
from jax import lax
from jax.experimental import pallas as pl
from jax.experimental.pallas import tpu as pltpu
from jax.sharding import PartitionSpec as P

LANES = 128
REACH = 2
SIDE = 2 * REACH + 1
MARGIN = 4
HALF = 256
LOG2E = math.log2(math.e)
VMEM = pl.BlockSpec(memory_space=pltpu.VMEM)
SMEM = pl.BlockSpec(memory_space=pltpu.SMEM)
HBM = pl.BlockSpec(memory_space=pltpu.HBM)
ANY = pl.BlockSpec(memory_space=pl.ANY)
NT = (((1,), (1,)), ((), ()))


def scored_round(frame, bits):
    return 1 ^ (frame >> bits[0] & 1) ^ (frame >> bits[1] & 1)


def split_rows(row):
    return jnp.concatenate(
        [row[:, i * LANES : (i + 1) * LANES] for i in range(row.shape[1] // LANES)], axis=0
    )


def join_rows(rows):
    return jnp.concatenate([rows[i : i + 1] for i in range(rows.shape[0])], axis=1)


def to_columns(rows):
    chunks = rows[0].shape[0]
    table = jnp.concatenate(rows, axis=0)
    spare = LANES - table.shape[0]
    table = jnp.concatenate([table, jnp.zeros((spare, LANES), jnp.float32)], axis=0).T
    return [
        jnp.concatenate(
            [table[:, n * chunks + i : n * chunks + i + 1] for i in range(chunks)], axis=0
        )
        for n in range(len(rows))
    ]


def one_hot(column, width):
    lanes = lax.broadcasted_iota(jnp.int32, (column.shape[0], width), 1).astype(jnp.float32)
    return jnp.where(lanes == column, 1.0, 0.0).astype(jnp.bfloat16)


def fine_point(cells, subs, coarse_width):
    return (
        2 * lax.div(cells, coarse_width) + lax.shift_right_logical(subs, 1),
        2 * lax.rem(cells, coarse_width) + jnp.bitwise_and(subs, 1),
    )


def write_payload(rnd, map_ref, cells_ref, subs_ref, counts_ref, pay_ref, band_ref):
    height, width, channels = map_ref.shape
    bands = band_ref.shape[1] // channels
    band = height // bands
    slots = cells_ref.shape[-1]
    coarse_width = width // 2
    for y in range(height):
        r, yl = divmod(y, band)
        band_ref[pl.ds(yl * width, width), pl.ds(r * channels, channels)] = map_ref[y]
    cells, subs = cells_ref[0, rnd], subs_ref[0, rnd]
    own, far = split_rows(cells[0:1]), split_rows(cells[1:2])
    own_y, own_x = fine_point(own, split_rows(subs[0:1]), coarse_width)
    far_y, far_x = fine_point(far, split_rows(subs[1:2]), coarse_width)
    count = jnp.where(rnd == 0, counts_ref[:, 0:1], counts_ref[:, 1:2])
    chunks = slots // LANES
    halves = jnp.broadcast_to(lax.div(count + (HALF - 1), HALF), (2 * chunks, LANES))
    pay_ref[pl.ds(slots, 4 * chunks), :] = (
        jnp.concatenate([far_y, far_x, halves], axis=0).astype(jnp.float32).astype(jnp.bfloat16)
    )
    rows = [own_x, lax.rem(own_y, band), lax.div(own_y, band)]
    x, in_band, which = to_columns([one.astype(jnp.float32) for one in rows])
    hot_x = one_hot(x, width)
    in_band = jnp.broadcast_to(in_band, hot_x.shape).astype(jnp.bfloat16)
    zero = jnp.zeros_like(hot_x)
    hot = jnp.concatenate([jnp.where(in_band == y, hot_x, zero) for y in range(band)], axis=1)
    got = jnp.dot(hot, band_ref[...], preferred_element_type=jnp.float32)
    query = jnp.zeros((slots, channels), jnp.float32)
    for r in range(bands):
        query = jnp.where(which == r, got[:, r * channels : (r + 1) * channels], query)
    for i in range(0, slots, LANES):
        pay_ref[pl.ds(i, LANES), :] = query[i : i + LANES].T.astype(jnp.bfloat16)


def list_kernel(bits, cells_ref, counts_ref, list_ref):
    rnd = 1 - scored_round(lax.axis_index("frame"), bits)
    count = jnp.where(rnd == 0, counts_ref[:, 0:1], counts_ref[:, 1:2])
    list_ref[0:2, :] = cells_ref[0, rnd]
    list_ref[2:4, :] = jnp.broadcast_to(count, (2, list_ref.shape[1]))


def query_kernel(bits, map_ref, cells_ref, subs_ref, counts_ref, pay_ref, tick_ref, band_ref):
    rnd = 1 - scored_round(lax.axis_index("frame"), bits)
    write_payload(rnd, map_ref, cells_ref, subs_ref, counts_ref, pay_ref, band_ref)
    tick_ref[...] = jnp.zeros_like(tick_ref)


def payload_ids(pay_ref):
    chunks = pay_ref.shape[0] // (LANES + 4)
    ids = pay_ref[pl.ds(chunks * LANES, 4 * chunks), :].astype(jnp.float32)
    both = jnp.max(ids[2 * chunks :]) > 1.5
    return join_rows(ids[:chunks]), join_rows(ids[chunks : 2 * chunks]), both


def fold(tok_ref, fold_ref):
    half, width = fold_ref.shape[0], tok_ref.shape[1]
    fold_ref[:, pl.ds(0, width)] = tok_ref[pl.ds(0, half), :]
    fold_ref[:, pl.ds(width, width)] = tok_ref[pl.ds(half, half), :]


def pick(fold_ref, column):
    half, width = fold_ref.shape[0], fold_ref.shape[1] // 2
    upper = column >= half
    got = jnp.dot(
        one_hot(jnp.where(upper, column - half, column), half),
        fold_ref[...],
        preferred_element_type=jnp.float32,
    )
    return jnp.where(upper, got[:, width:], got[:, :width])


def second_kernel(
    bits, cuts, tick_ref, map_ref, cells_ref, subs_ref, counts_ref, bands_ref, pay_ref, band_ref
):
    del tick_ref
    rnd = scored_round(lax.axis_index("frame"), bits)
    write_payload(rnd, map_ref, cells_ref, subs_ref, counts_ref, pay_ref, band_ref)
    height, width, channels = map_ref.shape
    cut_y, cut_x = cuts
    band, span = height // cut_y, width // cut_x
    wide = span + 2 * MARGIN
    blank = jnp.zeros((wide, channels), jnp.float32)
    edge = jnp.zeros((MARGIN, channels), jnp.float32)
    for r in range(cut_y):
        slabs = [[] for _ in range(cut_x)]
        for yl in range(band + 2 * REACH):
            y = r * band - REACH + yl
            if 0 <= y < height:
                row = jnp.concatenate([edge, map_ref[y].astype(jnp.float32), edge], axis=0)
            for c in range(cut_x):
                slabs[c].append(row[c * span : c * span + wide] if 0 <= y < height else blank)
        for c in range(cut_x):
            bands_ref[:, pl.ds((r * cut_x + c) * channels, channels)] = jnp.concatenate(
                slabs[c], axis=0
            ).astype(jnp.bfloat16)


def lane_sums(rows):
    return jnp.concatenate(
        [
            jnp.sum(rows[i : i + LANES].T, axis=0, keepdims=True)
            for i in range(0, rows.shape[0], LANES)
        ],
        axis=1,
    )


def scores_of(tok_ref, rows):
    return lax.dot_general(tok_ref[...], rows, NT, preferred_element_type=jnp.float32)


def exp_sums(tok_ref, rows, scale):
    expo = jnp.exp2(scores_of(tok_ref, rows) * (scale * LOG2E))
    return jnp.sum(expo, axis=0, keepdims=True)


def safe_lse(tok_ref, rows, scale):
    scores = scores_of(tok_ref, rows) * scale
    top = jnp.max(scores, axis=0, keepdims=True)
    return top + jnp.log(jnp.sum(jnp.exp(scores - top), axis=0, keepdims=True))


def conf_kernel(
    bits, scale, counts_ref, cells_ref, list_ref, tok_ref, far_tok_ref, conf_ref,
    mine_ref, theirs_ref, own_fold, far_fold, score_ref, sums_ref,
):
    tok_count = tok_ref.shape[0]
    slots = cells_ref.shape[-1]
    scored = scored_round(lax.axis_index("frame"), bits)
    fold(tok_ref, own_fold)
    fold(far_tok_ref, far_fold)
    here, there = cells_ref[0, scored], list_ref[0:2, :]
    columns = [here[0:1], here[1:2], there[0:1], there[1:2]]
    here_own, here_far, there_own, there_far = to_columns(
        [split_rows(row.astype(jnp.float32)) for row in columns]
    )
    own_cell = jnp.concatenate([here_own, there_far], axis=0)
    far_cell = jnp.concatenate([here_far, there_own], axis=0)
    score_ref[...] = jnp.zeros_like(score_ref)
    sums_ref[...] = jnp.ones_like(sums_ref)

    def tiles(starts):
        mine = [pick(own_fold, own_cell[i : i + HALF]) for i in starts]
        theirs = [pick(far_fold, far_cell[i : i + HALF]) for i in starts]
        one = [exp_sums(far_tok_ref, rows.astype(jnp.bfloat16), scale) for rows in mine]
        two = [exp_sums(tok_ref, rows.astype(jnp.bfloat16), scale) for rows in theirs]
        for n, i in enumerate(starts):
            rows = pl.ds(i, HALF)
            mine_ref[rows, :] = mine[n].astype(jnp.bfloat16)
            theirs_ref[rows, :] = theirs[n].astype(jnp.bfloat16)
            score_ref[:, rows] = lane_sums(mine[n] * theirs[n])
            sums_ref[0:1, rows] = one[n]
            sums_ref[1:2, rows] = two[n]

    def safe(starts):
        for i in starts:
            rows = pl.ds(i, HALF)
            sums_ref[0:1, rows] = safe_lse(far_tok_ref, mine_ref[rows, :], scale)
            sums_ref[1:2, rows] = safe_lse(tok_ref, theirs_ref[rows, :], scale)

    counts = jnp.where(scored == 0, counts_ref[:, 0:1], counts_ref[:, 1:2])
    here_more = jnp.max(counts) > HALF
    there_more = jnp.max(list_ref[2:3, :]) > HALF
    first = [0, slots]
    here_rest = list(range(HALF, slots, HALF))
    there_rest = [i + slots for i in here_rest]
    tiles(first)
    pl.when(here_more)(functools.partial(tiles, here_rest))
    pl.when(there_more)(functools.partial(tiles, there_rest))
    least = jnp.min(sums_ref[...])
    most = jnp.max(sums_ref[...])
    sums_ref[...] = jnp.log(sums_ref[...])

    @pl.when(jnp.logical_not((least > 1e-30) & (most < 1e30)))
    def _():
        safe(first)
        pl.when(here_more)(functools.partial(safe, here_rest))
        pl.when(there_more)(functools.partial(safe, there_rest))

    conf = score_ref[...] * (2.0 * scale) + 2.0 * math.log(tok_count)
    conf = conf - (sums_ref[0:1, :] + sums_ref[1:2, :])
    conf_ref[0:1, :] = conf[:, :slots]
    conf_ref[1:3, :] = jnp.broadcast_to(conf[:, slots:], (2, slots))


def heat_kernel(cuts, band, span, pay_ref, bands_ref, conf_ref, out_ref):
    cut_y, cut_x = cuts
    slots = conf_ref.shape[1]
    channels = pay_ref.shape[1]
    high, wide = band + 2 * REACH, span + 2 * MARGIN
    far_y, far_x, both = payload_ids(pay_ref)
    at_y = jnp.floor((far_y + 0.5) * (1.0 / band))
    at_x = jnp.floor((far_x + 0.5) * (1.0 / span))
    local_y = far_y - at_y * band + REACH
    local_x = far_x - at_x * span + MARGIN
    which = jnp.broadcast_to(at_y * cut_x + at_x, (channels, slots)).astype(jnp.bfloat16)
    scale = channels**-0.5 * LOG2E
    out_ref[2:3, :] = conf_ref[2:3, :]

    def windows(i):
        query = jnp.concatenate(
            [pay_ref[pl.ds(n, LANES), :] for n in range(i, i + HALF, LANES)], axis=1
        )
        zero = jnp.zeros_like(query)
        right = jnp.concatenate(
            [jnp.where(which[:, i : i + HALF] == n, query, zero) for n in range(cut_y * cut_x)],
            axis=0,
        )
        heat = jnp.dot(bands_ref[...], right, preferred_element_type=jnp.float32)
        ly = local_y[:, i : i + HALF].astype(jnp.int32)
        lx = local_x[:, i : i + HALF].astype(jnp.int32)
        shift_x = lax.broadcasted_iota(jnp.int32, (8, HALF), 0) - lx + REACH & 7
        tile_x = lx + shift_x - REACH >> 3
        rows = []
        for yl in range(high):
            found = heat[yl * wide : yl * wide + 8]
            for t in range(1, wide // 8):
                start = yl * wide + 8 * t
                found = jnp.where(tile_x == t, heat[start : start + 8], found)
            rows.append(found)
        kept, deltas = [], []
        for n in range(8):
            shift_y = n - ly + REACH & 7
            tile_y = ly + shift_y - REACH >> 3
            found = rows[n]
            for t, other in enumerate(rows[n + 8 :: 8]):
                found = jnp.where(tile_y == t + 1, other, found)
            keep = (shift_x < SIDE) & (shift_y < SIDE)
            kept.append(jnp.where(keep, found, -jnp.inf))
            deltas.append((shift_y - REACH).astype(jnp.float32))
        top = jnp.max(functools.reduce(jnp.maximum, kept), axis=0, keepdims=True)
        expos = [jnp.exp2((one - top) * scale) for one in kept]
        total = sum(expos[1:], expos[0])
        total_y = sum(expo * delta for expo, delta in zip(expos, deltas))
        whole = jnp.sum(total, axis=0, keepdims=True)
        delta_x = (shift_x - REACH).astype(jnp.float32)
        out_ref[0:1, pl.ds(i, HALF)] = jnp.sum(total * delta_x, axis=0, keepdims=True) / whole
        out_ref[1:2, pl.ds(i, HALF)] = jnp.sum(total_y, axis=0, keepdims=True) / whole

    @pl.when(jnp.logical_not(both))
    def _():
        out_ref[0:2, :] = jnp.zeros((2, slots), jnp.float32)
        windows(0)

    @pl.when(both)
    def _():
        for i in range(0, slots, HALF):
            windows(i)


def early_kernel(bits, counts_ref, conf_ref, got_ref, conf_out, base_ref):
    scored = scored_round(lax.axis_index("frame"), bits)
    slots = conf_ref.shape[1]
    lane = lax.broadcasted_iota(jnp.int32, (1, slots), 1)
    for rnd in range(2):
        valid = lane < counts_ref[:, rnd : rnd + 1]
        mine = scored == rnd
        conf = jnp.where(mine, conf_ref[0:1, :], got_ref[2:3, :])
        conf_out[0, rnd : rnd + 1, :] = jnp.where(valid, conf, 0.0)
        offs = jnp.where(mine, 0.0, got_ref[0:2, :])
        base_ref[2 * rnd : 2 * rnd + 2, :] = jnp.where(valid, offs, 0.0)
        base_ref[4 + rnd : 5 + rnd, :] = jnp.where(valid & mine, 1.0, 0.0)


def late_kernel(base_ref, got_ref, offs_out):
    for rnd in range(2):
        valid = base_ref[4 + rnd : 5 + rnd, :] > 0.5
        base = base_ref[2 * rnd : 2 * rnd + 2, :]
        offs_out[0, rnd] = jnp.where(valid, got_ref[0:2, :], base)


def body(tokens, fine_map, matches, subcells, counts):
    frames = lax.axis_size("frame")
    top = frames.bit_length() - 1
    bits = [top - 1 - rnd for rnd in range(matches.shape[1])]
    slots = matches.shape[3]
    tok_count, width = tokens.shape
    height, fine_width, channels = fine_map.shape
    bands = math.gcd(height, 4)
    cuts = (math.gcd(height, 2), math.gcd(fine_width, 2))
    band, span = height // cuts[0], fine_width // cuts[1]
    cells = (band + 2 * REACH) * (span + 2 * MARGIN)
    tiles = cuts[0] * cuts[1]
    id_rows = 4 * slots // LANES
    f32, bf16 = jnp.float32, jnp.bfloat16

    sends = [(i, i ^ 1 << bits[1 - scored_round(i, bits)]) for i in range(frames)]
    backs = [(b, a) for a, b in sends]
    scale = 10.0 / width
    small = pltpu.CompilerParams(vmem_limit_bytes=24 << 20)

    def hint(flops, moved=0):
        return pl.CostEstimate(flops=flops, bytes_accessed=moved, transcendentals=0)

    far_tokens = lax.ppermute(tokens, "frame", sends)
    far_list = pl.pallas_call(
        functools.partial(list_kernel, bits),
        out_shape=jax.ShapeDtypeStruct((4, slots), jnp.int32),
        in_specs=[VMEM] * 2,
        out_specs=VMEM,
        name="scored_list",
        cost_estimate=hint(1 << 34),
        compiler_params=small,
    )(matches, counts)
    far_list = lax.ppermute(far_list, "frame", sends)
    payload = jax.ShapeDtypeStruct((slots + id_rows, channels), bf16)
    map_rows = pltpu.VMEM((height // bands * fine_width, bands * channels), bf16)
    pay_a, tick = pl.pallas_call(
        functools.partial(query_kernel, bits),
        out_shape=(payload, jax.ShapeDtypeStruct((8, LANES), f32)),
        in_specs=[VMEM] * 4,
        out_specs=(VMEM,) * 2,
        scratch_shapes=[map_rows],
        name="queries_a",
        cost_estimate=hint(1 << 30),
        compiler_params=small,
    )(fine_map, matches, subcells, counts)
    pay_a = lax.ppermute(pay_a, "frame", sends)
    band_map, pay_b = pl.pallas_call(
        functools.partial(second_kernel, bits, cuts),
        out_shape=(jax.ShapeDtypeStruct((cells, tiles * channels), bf16), payload),
        in_specs=[ANY] + [VMEM] * 4,
        out_specs=(VMEM,) * 2,
        scratch_shapes=[map_rows],
        name="queries_b",
        compiler_params=small,
    )(tick, fine_map, matches, subcells, counts)
    pay_b = lax.ppermute(pay_b, "frame", backs)

    conf = pl.pallas_call(
        functools.partial(conf_kernel, bits, scale),
        out_shape=jax.ShapeDtypeStruct((3, slots), f32),
        in_specs=[VMEM] * 5,
        out_specs=VMEM,
        scratch_shapes=[pltpu.VMEM((2 * slots, width), bf16)] * 2
        + [pltpu.VMEM((tok_count // 2, 2 * width), bf16)] * 2
        + [pltpu.VMEM((1, 2 * slots), f32), pltpu.VMEM((2, 2 * slots), f32)],
        name="confidences",
        cost_estimate=hint(1 << 34),
        compiler_params=small,
    )(counts, matches, far_list, tokens, far_tokens)

    def windows(pay, conf):
        return pl.pallas_call(
            functools.partial(heat_kernel, cuts, band, span),
            out_shape=jax.ShapeDtypeStruct((3, slots), f32),
            in_specs=[VMEM] * 3,
            out_specs=VMEM,
            name="window_offsets",
            cost_estimate=hint(1 << 33, 2 * cells * tiles * channels),
            compiler_params=small,
        )(pay, band_map, conf)

    answer_a = windows(pay_a, conf)
    got_a = lax.ppermute(answer_a, "frame", backs)
    answer_b = windows(pay_b, answer_a)
    got_b = lax.ppermute(answer_b, "frame", sends)

    rounds = len(bits)
    conf_out, base = pl.pallas_call(
        functools.partial(early_kernel, bits),
        out_shape=(
            jax.ShapeDtypeStruct((1, rounds, slots), f32),
            jax.ShapeDtypeStruct((3 * rounds, slots), f32),
        ),
        in_specs=[VMEM] * 3,
        out_specs=(VMEM,) * 2,
        name="early_outputs",
        compiler_params=small,
    )(counts, conf, got_a)
    offs_out = pl.pallas_call(
        late_kernel,
        out_shape=jax.ShapeDtypeStruct((1, rounds, 2, slots), f32),
        in_specs=[VMEM] * 2,
        out_specs=VMEM,
        name="late_outputs",
        compiler_params=small,
    )(base, got_b)
    return conf_out, offs_out


def solution(mesh):
    return jax.shard_map(
        body,
        mesh=mesh,
        in_specs=(
            P("frame", None),
            P("frame", None, None),
            P("frame", None, None, None),
            P("frame", None, None, None),
            P("frame", None),
        ),
        out_specs=(P("frame", None, None), P("frame", None, None, None)),
        check_vma=False,
    )
```

```python
import functools
import math

import jax
import jax.numpy as jnp
from jax import lax
from jax.experimental import pallas as pl
from jax.experimental.pallas import tpu as pltpu
from jax.sharding import PartitionSpec as P

LANES = 128
REACH = 2
SIDE = 2 * REACH + 1
MARGIN = 4
HALF = 256
LOG2E = math.log2(math.e)
VMEM = pl.BlockSpec(memory_space=pltpu.VMEM)
SMEM = pl.BlockSpec(memory_space=pltpu.SMEM)
HBM = pl.BlockSpec(memory_space=pltpu.HBM)
ANY = pl.BlockSpec(memory_space=pl.ANY)
NT = (((1,), (1,)), ((), ()))


def scored_round(frame, bits):
    return 1 ^ (frame >> bits[0] & 1) ^ (frame >> bits[1] & 1)


def split_rows(row):
    return jnp.concatenate(
        [row[:, i * LANES : (i + 1) * LANES] for i in range(row.shape[1] // LANES)], axis=0
    )


def join_rows(rows):
    return jnp.concatenate([rows[i : i + 1] for i in range(rows.shape[0])], axis=1)


def to_columns(rows):
    chunks = rows[0].shape[0]
    table = jnp.concatenate(rows, axis=0)
    spare = LANES - table.shape[0]
    table = jnp.concatenate([table, jnp.zeros((spare, LANES), jnp.float32)], axis=0).T
    return [
        jnp.concatenate(
            [table[:, n * chunks + i : n * chunks + i + 1] for i in range(chunks)], axis=0
        )
        for n in range(len(rows))
    ]


def one_hot(column, width):
    lanes = lax.broadcasted_iota(jnp.int32, (column.shape[0], width), 1).astype(jnp.float32)
    return jnp.where(lanes == column, 1.0, 0.0).astype(jnp.bfloat16)


def fine_point(cells, subs, coarse_width):
    return (
        2 * lax.div(cells, coarse_width) + lax.shift_right_logical(subs, 1),
        2 * lax.rem(cells, coarse_width) + jnp.bitwise_and(subs, 1),
    )


def payload_of(rnd, cells_ref, subs_ref, counts_ref, band_ref, channels, band):
    slots = cells_ref.shape[-1]
    width = band_ref.shape[0] // band
    coarse_width = width // 2
    bands = band_ref.shape[1] // channels
    cells, subs = cells_ref[0, rnd], subs_ref[0, rnd]
    own, far = split_rows(cells[0:1]), split_rows(cells[1:2])
    own_y, own_x = fine_point(own, split_rows(subs[0:1]), coarse_width)
    far_y, far_x = fine_point(far, split_rows(subs[1:2]), coarse_width)
    count = jnp.where(rnd == 0, counts_ref[:, 0:1], counts_ref[:, 1:2])
    chunks = slots // LANES
    halves = jnp.broadcast_to(lax.div(count + (HALF - 1), HALF), (2 * chunks, LANES))
    ids = jnp.concatenate([far_y, far_x, halves], axis=0)
    rows = [own_x, lax.rem(own_y, band), lax.div(own_y, band)]
    x, in_band, which = to_columns([one.astype(jnp.float32) for one in rows])
    hot_x = one_hot(x, width)
    in_band = jnp.broadcast_to(in_band, hot_x.shape).astype(jnp.bfloat16)
    zero = jnp.zeros_like(hot_x)
    hot = jnp.concatenate([jnp.where(in_band == y, hot_x, zero) for y in range(band)], axis=1)
    got = jnp.dot(hot, band_ref[...], preferred_element_type=jnp.float32)
    query = jnp.zeros((slots, channels), jnp.float32)
    for r in range(bands):
        query = jnp.where(which == r, got[:, r * channels : (r + 1) * channels], query)
    blocks = [query[i : i + LANES].T.astype(jnp.bfloat16) for i in range(0, slots, LANES)]
    return blocks, ids.astype(jnp.float32).astype(jnp.bfloat16)


def list_kernel(bits, cells_ref, counts_ref, list_ref):
    rnd = 1 - scored_round(lax.axis_index("frame"), bits)
    count = jnp.where(rnd == 0, counts_ref[:, 0:1], counts_ref[:, 1:2])
    list_ref[0:2, :] = cells_ref[0, rnd]
    list_ref[2:4, :] = jnp.broadcast_to(count, (2, list_ref.shape[1]))


def query_kernel(
    bits, map_ref, cells_ref, subs_ref, counts_ref, pay_a_ref, pay_b_ref, rest_b_ref, band_ref
):
    height, width, channels = map_ref.shape
    bands = band_ref.shape[1] // channels
    band = height // bands
    for y in range(height):
        r, yl = divmod(y, band)
        band_ref[pl.ds(yl * width, width), pl.ds(r * channels, channels)] = map_ref[y]
    scored = scored_round(lax.axis_index("frame"), bits)
    parts = (cells_ref, subs_ref, counts_ref, band_ref, channels, band)
    blocks, ids = payload_of(1 - scored, *parts)
    pay_a_ref[...] = jnp.concatenate(blocks + [ids], axis=0)
    blocks, ids = payload_of(scored, *parts)
    half = HALF // LANES
    pay_b_ref[...] = jnp.concatenate(blocks[:half] + [ids], axis=0)
    rest_b_ref[...] = jnp.concatenate(blocks[half:], axis=0)


def payload_ids(pay_ref, slots):
    chunks = slots // LANES
    rows = 4 * chunks
    ids = pay_ref[pl.ds(pay_ref.shape[0] - rows, rows), :].astype(jnp.float32)
    both = jnp.max(ids[2 * chunks :]) > 1.5
    return join_rows(ids[:chunks]), join_rows(ids[chunks : 2 * chunks]), both


def fold(tok_ref, fold_ref):
    half, width = fold_ref.shape[0], tok_ref.shape[1]
    fold_ref[:, pl.ds(0, width)] = tok_ref[pl.ds(0, half), :]
    fold_ref[:, pl.ds(width, width)] = tok_ref[pl.ds(half, half), :]


def pick(fold_ref, column):
    half, width = fold_ref.shape[0], fold_ref.shape[1] // 2
    upper = column >= half
    got = jnp.dot(
        one_hot(jnp.where(upper, column - half, column), half),
        fold_ref[...],
        preferred_element_type=jnp.float32,
    )
    return jnp.where(upper, got[:, width:], got[:, :width])


def fill_bands(r, cuts, map_ref, bands_ref):
    height, width, channels = map_ref.shape
    cut_y, cut_x = cuts
    band, span = height // cut_y, width // cut_x
    wide = span + 2 * MARGIN
    blank = jnp.zeros((wide, channels), jnp.float32)
    edge = jnp.zeros((MARGIN, channels), jnp.float32)
    slabs = [[] for _ in range(cut_x)]
    for yl in range(band + 2 * REACH):
        y = r * band - REACH + yl
        if 0 <= y < height:
            row = jnp.concatenate([edge, map_ref[y].astype(jnp.float32), edge], axis=0)
        for c in range(cut_x):
            slabs[c].append(row[c * span : c * span + wide] if 0 <= y < height else blank)
    for c in range(cut_x):
        bands_ref[:, pl.ds((r * cut_x + c) * channels, channels)] = jnp.concatenate(
            slabs[c], axis=0
        ).astype(jnp.bfloat16)


def band_kernel(cuts, map_ref, pay_in, bands_ref, pay_ref):
    del pay_in, pay_ref
    fill_bands(0, cuts, map_ref, bands_ref)


def more_bands_kernel(cuts, map_ref, bands_in, rest_in, bands_ref, rest_ref):
    del bands_in, rest_in, rest_ref
    for r in range(1, cuts[0]):
        fill_bands(r, cuts, map_ref, bands_ref)


def lane_sums(rows):
    return jnp.concatenate(
        [
            jnp.sum(rows[i : i + LANES].T, axis=0, keepdims=True)
            for i in range(0, rows.shape[0], LANES)
        ],
        axis=1,
    )


def scores_of(tok_ref, rows):
    return lax.dot_general(tok_ref[...], rows, NT, preferred_element_type=jnp.float32)


def exp_sums(tok_ref, rows, scale):
    expo = jnp.exp2(scores_of(tok_ref, rows) * (scale * LOG2E))
    return jnp.sum(expo, axis=0, keepdims=True)


def safe_lse(tok_ref, rows, scale):
    scores = scores_of(tok_ref, rows) * scale
    top = jnp.max(scores, axis=0, keepdims=True)
    return top + jnp.log(jnp.sum(jnp.exp(scores - top), axis=0, keepdims=True))


def conf_kernel(
    bits, scale, counts_ref, cells_ref, list_ref, tok_ref, far_tok_ref, conf_ref,
    mine_ref, theirs_ref, own_fold, far_fold, score_ref, sums_ref,
):
    tok_count = tok_ref.shape[0]
    slots = cells_ref.shape[-1]
    scored = scored_round(lax.axis_index("frame"), bits)
    fold(tok_ref, own_fold)
    fold(far_tok_ref, far_fold)
    here, there = cells_ref[0, scored], list_ref[0:2, :]
    columns = [here[0:1], here[1:2], there[0:1], there[1:2]]
    here_own, here_far, there_own, there_far = to_columns(
        [split_rows(row.astype(jnp.float32)) for row in columns]
    )
    own_cell = jnp.concatenate([here_own, there_far], axis=0)
    far_cell = jnp.concatenate([here_far, there_own], axis=0)
    score_ref[...] = jnp.zeros_like(score_ref)
    sums_ref[...] = jnp.ones_like(sums_ref)

    def tiles(starts):
        mine = [pick(own_fold, own_cell[i : i + HALF]) for i in starts]
        theirs = [pick(far_fold, far_cell[i : i + HALF]) for i in starts]
        one = [exp_sums(far_tok_ref, rows.astype(jnp.bfloat16), scale) for rows in mine]
        two = [exp_sums(tok_ref, rows.astype(jnp.bfloat16), scale) for rows in theirs]
        for n, i in enumerate(starts):
            rows = pl.ds(i, HALF)
            mine_ref[rows, :] = mine[n].astype(jnp.bfloat16)
            theirs_ref[rows, :] = theirs[n].astype(jnp.bfloat16)
            score_ref[:, rows] = lane_sums(mine[n] * theirs[n])
            sums_ref[0:1, rows] = one[n]
            sums_ref[1:2, rows] = two[n]

    def safe(starts):
        for i in starts:
            rows = pl.ds(i, HALF)
            sums_ref[0:1, rows] = safe_lse(far_tok_ref, mine_ref[rows, :], scale)
            sums_ref[1:2, rows] = safe_lse(tok_ref, theirs_ref[rows, :], scale)

    counts = jnp.where(scored == 0, counts_ref[:, 0:1], counts_ref[:, 1:2])
    here_more = jnp.max(counts) > HALF
    there_more = jnp.max(list_ref[2:3, :]) > HALF
    first = [0, slots]
    here_rest = list(range(HALF, slots, HALF))
    there_rest = [i + slots for i in here_rest]
    only_here = here_more & jnp.logical_not(there_more)
    only_there = there_more & jnp.logical_not(here_more)
    tiles(first)
    pl.when(only_here)(functools.partial(tiles, here_rest))
    pl.when(only_there)(functools.partial(tiles, there_rest))
    pl.when(here_more & there_more)(functools.partial(tiles, here_rest + there_rest))
    least = jnp.min(sums_ref[...])
    most = jnp.max(sums_ref[...])
    sums_ref[...] = jnp.log(sums_ref[...])

    @pl.when(jnp.logical_not((least > 1e-30) & (most < 1e30)))
    def _():
        safe(first)
        pl.when(here_more)(functools.partial(safe, here_rest))
        pl.when(there_more)(functools.partial(safe, there_rest))

    conf = score_ref[...] * (2.0 * scale) + 2.0 * math.log(tok_count)
    conf = conf - (sums_ref[0:1, :] + sums_ref[1:2, :])
    conf_ref[0:1, :] = conf[:, :slots]
    conf_ref[1:3, :] = jnp.broadcast_to(conf[:, slots:], (2, slots))


def window_offsets(geometry, pay_ref, start, far_y, far_x, bands_ref):
    cut_y, cut_x, band, span = geometry
    high, wide = band + 2 * REACH, span + 2 * MARGIN
    query = jnp.concatenate(
        [pay_ref[pl.ds(start + n, LANES), :] for n in range(0, HALF, LANES)], axis=1
    )
    scale = query.shape[0] ** -0.5 * LOG2E
    at_y = jnp.floor((far_y + 0.5) * (1.0 / band))
    at_x = jnp.floor((far_x + 0.5) * (1.0 / span))
    ly = (far_y - at_y * band + REACH).astype(jnp.int32)
    lx = (far_x - at_x * span + MARGIN).astype(jnp.int32)
    which = jnp.broadcast_to(at_y * cut_x + at_x, query.shape).astype(jnp.bfloat16)
    zero = jnp.zeros_like(query)
    right = jnp.concatenate(
        [jnp.where(which == n, query, zero) for n in range(cut_y * cut_x)], axis=0
    )
    heat = jnp.dot(bands_ref[...], right, preferred_element_type=jnp.float32)
    shift_x = lax.broadcasted_iota(jnp.int32, (8, HALF), 0) - lx + REACH & 7
    tile_x = lx + shift_x - REACH >> 3
    rows = []
    for yl in range(high):
        found = heat[yl * wide : yl * wide + 8]
        for t in range(1, wide // 8):
            begin = yl * wide + 8 * t
            found = jnp.where(tile_x == t, heat[begin : begin + 8], found)
        rows.append(found)
    kept, deltas = [], []
    for n in range(8):
        shift_y = n - ly + REACH & 7
        tile_y = ly + shift_y - REACH >> 3
        found = rows[n]
        for t, other in enumerate(rows[n + 8 :: 8]):
            found = jnp.where(tile_y == t + 1, other, found)
        keep = (shift_x < SIDE) & (shift_y < SIDE)
        kept.append(jnp.where(keep, found, -jnp.inf))
        deltas.append((shift_y - REACH).astype(jnp.float32))
    top = jnp.max(functools.reduce(jnp.maximum, kept), axis=0, keepdims=True)
    expos = [jnp.exp2((one - top) * scale) for one in kept]
    total = sum(expos[1:], expos[0])
    total_y = sum(expo * delta for expo, delta in zip(expos, deltas))
    whole = jnp.sum(total, axis=0, keepdims=True)
    delta_x = (shift_x - REACH).astype(jnp.float32)
    sum_x = jnp.sum(total * delta_x, axis=0, keepdims=True)
    return sum_x / whole, jnp.sum(total_y, axis=0, keepdims=True) / whole


def store_windows(geometry, pay_ref, start, i, far_y, far_x, bands_ref, out_ref):
    part = slice(i, i + HALF)
    off_x, off_y = window_offsets(
        geometry, pay_ref, start, far_y[:, part], far_x[:, part], bands_ref
    )
    out_ref[0:1, pl.ds(i, HALF)] = off_x
    out_ref[1:2, pl.ds(i, HALF)] = off_y


def heat_kernel(geometry, pay_ref, bands_ref, conf_ref, out_ref):
    slots = conf_ref.shape[1]
    far_y, far_x, both = payload_ids(pay_ref, slots)
    out_ref[2:3, :] = conf_ref[2:3, :]

    def store(i):
        store_windows(geometry, pay_ref, i, i, far_y, far_x, bands_ref, out_ref)

    @pl.when(jnp.logical_not(both))
    def _():
        out_ref[0:2, :] = jnp.zeros((2, slots), jnp.float32)
        store(0)

    @pl.when(both)
    def _():
        for i in range(0, slots, HALF):
            store(i)


def is_early(bits):
    frame = lax.axis_index("frame")
    return ((frame >> bits[0] & 1) + (frame >> bits[1] & 1)) == 0


def before_kernel(geometry, bits, pay_ref, bands_ref, answer_ref, answer_out, out_ref):
    slots = answer_ref.shape[1]
    answer_out[...] = answer_ref[...]
    out_ref[...] = jnp.zeros_like(out_ref)

    @pl.when(is_early(bits))
    def _():
        far_y, far_x, _ = payload_ids(pay_ref, slots)
        store_windows(geometry, pay_ref, 0, 0, far_y, far_x, bands_ref, out_ref)


def after_kernel(geometry, bits, pay_ref, bands_ref, held_ref, out_ref):
    slots = held_ref.shape[1]
    out_ref[...] = held_ref[...]

    @pl.when(jnp.logical_not(is_early(bits)))
    def _():
        far_y, far_x, _ = payload_ids(pay_ref, slots)
        store_windows(geometry, pay_ref, 0, 0, far_y, far_x, bands_ref, out_ref)


def rest_kernel(geometry, pay_ref, rest_ref, bands_ref, held_ref, out_ref):
    slots = held_ref.shape[1]
    far_y, far_x, both = payload_ids(pay_ref, slots)
    out_ref[...] = held_ref[...]

    @pl.when(both)
    def _():
        for i in range(HALF, slots, HALF):
            store_windows(geometry, rest_ref, i - HALF, i, far_y, far_x, bands_ref, out_ref)


def early_kernel(bits, counts_ref, conf_ref, got_ref, conf_out, base_ref):
    scored = scored_round(lax.axis_index("frame"), bits)
    slots = conf_ref.shape[1]
    lane = lax.broadcasted_iota(jnp.int32, (1, slots), 1)
    for rnd in range(2):
        valid = lane < counts_ref[:, rnd : rnd + 1]
        mine = scored == rnd
        conf = jnp.where(mine, conf_ref[0:1, :], got_ref[2:3, :])
        conf_out[0, rnd : rnd + 1, :] = jnp.where(valid, conf, 0.0)
        offs = jnp.where(mine, 0.0, got_ref[0:2, :])
        base_ref[2 * rnd : 2 * rnd + 2, :] = jnp.where(valid, offs, 0.0)
        base_ref[4 + rnd : 5 + rnd, :] = jnp.where(valid & mine, 1.0, 0.0)


def late_kernel(base_ref, got_ref, offs_out):
    for rnd in range(2):
        valid = base_ref[4 + rnd : 5 + rnd, :] > 0.5
        base = base_ref[2 * rnd : 2 * rnd + 2, :]
        offs_out[0, rnd] = jnp.where(valid, got_ref[0:2, :], base)


def body(tokens, fine_map, matches, subcells, counts):
    frames = lax.axis_size("frame")
    top = frames.bit_length() - 1
    bits = [top - 1 - rnd for rnd in range(matches.shape[1])]
    slots = matches.shape[3]
    tok_count, width = tokens.shape
    height, fine_width, channels = fine_map.shape
    bands = math.gcd(height, 4)
    cuts = (math.gcd(height, 2), math.gcd(fine_width, 2))
    band, span = height // cuts[0], fine_width // cuts[1]
    cells = (band + 2 * REACH) * (span + 2 * MARGIN)
    tiles = cuts[0] * cuts[1]
    id_rows = 4 * slots // LANES
    f32, bf16 = jnp.float32, jnp.bfloat16

    sends = [(i, i ^ 1 << bits[1 - scored_round(i, bits)]) for i in range(frames)]
    backs = [(b, a) for a, b in sends]
    scale = 10.0 / width
    small = pltpu.CompilerParams(vmem_limit_bytes=24 << 20)

    def hint(flops, moved=0):
        return pl.CostEstimate(flops=flops, bytes_accessed=moved, transcendentals=0)

    far_tokens = lax.ppermute(tokens, "frame", sends)
    far_list = pl.pallas_call(
        functools.partial(list_kernel, bits),
        out_shape=jax.ShapeDtypeStruct((4, slots), jnp.int32),
        in_specs=[VMEM] * 2,
        out_specs=VMEM,
        name="scored_list",
        cost_estimate=hint(1 << 34),
        compiler_params=small,
    )(matches, counts)
    far_list = lax.ppermute(far_list, "frame", sends)
    payload = jax.ShapeDtypeStruct((slots + id_rows, channels), bf16)
    map_rows = pltpu.VMEM((height // bands * fine_width, bands * channels), bf16)
    pay_a, pay_b, rest_b = pl.pallas_call(
        functools.partial(query_kernel, bits),
        out_shape=(
            payload,
            jax.ShapeDtypeStruct((HALF + id_rows, channels), bf16),
            jax.ShapeDtypeStruct((slots - HALF, channels), bf16),
        ),
        in_specs=[VMEM] * 4,
        out_specs=(VMEM,) * 3,
        scratch_shapes=[map_rows],
        name="queries_a",
        cost_estimate=hint(1 << 30),
        compiler_params=small,
    )(fine_map, matches, subcells, counts)
    pay_a = lax.ppermute(pay_a, "frame", sends)
    band_shape = jax.ShapeDtypeStruct((cells, tiles * channels), bf16)
    band_map, pay_b = pl.pallas_call(
        functools.partial(band_kernel, cuts),
        out_shape=(band_shape, jax.ShapeDtypeStruct(pay_b.shape, bf16)),
        in_specs=[VMEM, ANY],
        out_specs=(VMEM, ANY),
        input_output_aliases={1: 1},
        name="bands",
        compiler_params=small,
    )(fine_map, pay_b)
    pay_b = lax.ppermute(pay_b, "frame", backs)
    band_map, rest_b = pl.pallas_call(
        functools.partial(more_bands_kernel, cuts),
        out_shape=(band_shape, jax.ShapeDtypeStruct(rest_b.shape, bf16)),
        in_specs=[VMEM, VMEM, ANY],
        out_specs=(VMEM, ANY),
        input_output_aliases={1: 0, 2: 1},
        name="bands_more",
        compiler_params=small,
    )(fine_map, band_map, rest_b)
    rest_b = lax.ppermute(rest_b, "frame", backs)

    conf = pl.pallas_call(
        functools.partial(conf_kernel, bits, scale),
        out_shape=jax.ShapeDtypeStruct((3, slots), f32),
        in_specs=[VMEM] * 5,
        out_specs=VMEM,
        scratch_shapes=[pltpu.VMEM((2 * slots, width), bf16)] * 2
        + [pltpu.VMEM((tok_count // 2, 2 * width), bf16)] * 2
        + [pltpu.VMEM((1, 2 * slots), f32), pltpu.VMEM((2, 2 * slots), f32)],
        name="confidences",
        cost_estimate=hint(1 << 34),
        compiler_params=small,
    )(counts, matches, far_list, tokens, far_tokens)

    geometry = (*cuts, band, span)
    answer = jax.ShapeDtypeStruct((3, slots), f32)

    def windows(kernel, name, outs, flops, *operands):
        return pl.pallas_call(
            kernel,
            out_shape=(answer,) * outs if outs > 1 else answer,
            in_specs=[VMEM] * len(operands),
            out_specs=(VMEM,) * outs if outs > 1 else VMEM,
            name=name,
            cost_estimate=hint(flops),
            compiler_params=small,
        )(*operands)

    answer_a = windows(
        functools.partial(heat_kernel, geometry), "windows_a", 1, 1 << 33, pay_a, band_map, conf
    )
    answer_a, held = windows(
        functools.partial(before_kernel, geometry, bits),
        "windows_before", 2, 1 << 28, pay_b, band_map, answer_a,
    )
    got_a = lax.ppermute(answer_a, "frame", backs)
    held = windows(
        functools.partial(after_kernel, geometry, bits),
        "windows_after", 1, 1 << 33, pay_b, band_map, held,
    )
    answer_b = windows(
        functools.partial(rest_kernel, geometry),
        "windows_rest", 1, 1 << 30, pay_b, rest_b, band_map, held,
    )
    got_b = lax.ppermute(answer_b, "frame", sends)

    rounds = len(bits)
    conf_out, base = pl.pallas_call(
        functools.partial(early_kernel, bits),
        out_shape=(
            jax.ShapeDtypeStruct((1, rounds, slots), f32),
            jax.ShapeDtypeStruct((3 * rounds, slots), f32),
        ),
        in_specs=[VMEM] * 3,
        out_specs=(VMEM,) * 2,
        name="early_outputs",
        compiler_params=small,
    )(counts, conf, got_a)
    offs_out = pl.pallas_call(
        late_kernel,
        out_shape=jax.ShapeDtypeStruct((1, rounds, 2, slots), f32),
        in_specs=[VMEM] * 2,
        out_specs=VMEM,
        name="late_outputs",
        compiler_params=small,
    )(base, got_b)
    return conf_out, offs_out


def solution(mesh):
    return jax.shard_map(
        body,
        mesh=mesh,
        in_specs=(
            P("frame", None),
            P("frame", None, None),
            P("frame", None, None, None),
            P("frame", None, None, None),
            P("frame", None),
        ),
        out_specs=(P("frame", None, None), P("frame", None, None, None)),
        check_vma=False,
    )
```

```python
import functools
import math

import jax
import jax.numpy as jnp
from jax import lax
from jax.experimental import pallas as pl
from jax.experimental.pallas import tpu as pltpu
from jax.sharding import PartitionSpec as P

LANES = 128
REACH = 2
SIDE = 2 * REACH + 1
MARGIN = 4
HALF = 256
LOG2E = math.log2(math.e)
VMEM = pl.BlockSpec(memory_space=pltpu.VMEM)
SMEM = pl.BlockSpec(memory_space=pltpu.SMEM)
HBM = pl.BlockSpec(memory_space=pltpu.HBM)
ANY = pl.BlockSpec(memory_space=pl.ANY)
NT = (((1,), (1,)), ((), ()))


def scored_round(frame, bits):
    return 1 ^ (frame >> bits[0] & 1) ^ (frame >> bits[1] & 1)


def split_rows(row):
    return jnp.concatenate(
        [row[:, i * LANES : (i + 1) * LANES] for i in range(row.shape[1] // LANES)], axis=0
    )


def join_rows(rows):
    return jnp.concatenate([rows[i : i + 1] for i in range(rows.shape[0])], axis=1)


def to_columns(rows):
    chunks = rows[0].shape[0]
    table = jnp.concatenate(rows, axis=0)
    spare = LANES - table.shape[0]
    table = jnp.concatenate([table, jnp.zeros((spare, LANES), jnp.float32)], axis=0).T
    return [
        jnp.concatenate(
            [table[:, n * chunks + i : n * chunks + i + 1] for i in range(chunks)], axis=0
        )
        for n in range(len(rows))
    ]


def one_hot(column, width):
    lanes = lax.broadcasted_iota(jnp.int32, (column.shape[0], width), 1).astype(jnp.float32)
    return jnp.where(lanes == column, 1.0, 0.0).astype(jnp.bfloat16)


def fine_point(cells, subs, coarse_width):
    return (
        2 * lax.div(cells, coarse_width) + lax.shift_right_logical(subs, 1),
        2 * lax.rem(cells, coarse_width) + jnp.bitwise_and(subs, 1),
    )


def write_payload(rnd, cells_ref, subs_ref, counts_ref, pay_ref, band_ref, band):
    slots = cells_ref.shape[-1]
    width = band_ref.shape[0] // band
    coarse_width = width // 2
    channels = pay_ref.shape[1]
    bands = band_ref.shape[1] // channels
    cells, subs = cells_ref[0, rnd], subs_ref[0, rnd]
    own, far = split_rows(cells[0:1]), split_rows(cells[1:2])
    own_y, own_x = fine_point(own, split_rows(subs[0:1]), coarse_width)
    far_y, far_x = fine_point(far, split_rows(subs[1:2]), coarse_width)
    count = jnp.where(rnd == 0, counts_ref[:, 0:1], counts_ref[:, 1:2])
    chunks = slots // LANES
    halves = jnp.broadcast_to(lax.div(count + (HALF - 1), HALF), (2 * chunks, LANES))
    pay_ref[pl.ds(slots, 4 * chunks), :] = (
        jnp.concatenate([far_y, far_x, halves], axis=0).astype(jnp.float32).astype(jnp.bfloat16)
    )
    rows = [own_x, lax.rem(own_y, band), lax.div(own_y, band)]
    x, in_band, which = to_columns([one.astype(jnp.float32) for one in rows])
    hot_x = one_hot(x, width)
    in_band = jnp.broadcast_to(in_band, hot_x.shape).astype(jnp.bfloat16)
    zero = jnp.zeros_like(hot_x)
    hot = jnp.concatenate([jnp.where(in_band == y, hot_x, zero) for y in range(band)], axis=1)
    got = jnp.dot(hot, band_ref[...], preferred_element_type=jnp.float32)
    query = jnp.zeros((slots, channels), jnp.float32)
    for r in range(bands):
        query = jnp.where(which == r, got[:, r * channels : (r + 1) * channels], query)
    for i in range(0, slots, LANES):
        pay_ref[pl.ds(i, LANES), :] = query[i : i + LANES].T.astype(jnp.bfloat16)


def list_kernel(bits, cells_ref, counts_ref, list_ref):
    rnd = 1 - scored_round(lax.axis_index("frame"), bits)
    count = jnp.where(rnd == 0, counts_ref[:, 0:1], counts_ref[:, 1:2])
    list_ref[0:2, :] = cells_ref[0, rnd]
    list_ref[2:4, :] = jnp.broadcast_to(count, (2, list_ref.shape[1]))


def query_kernel(
    bits, map_ref, cells_ref, subs_ref, counts_ref, pay_a_ref, pay_b_ref, band_ref
):
    height, width, channels = map_ref.shape
    bands = band_ref.shape[1] // channels
    band = height // bands
    for y in range(height):
        r, yl = divmod(y, band)
        band_ref[pl.ds(yl * width, width), pl.ds(r * channels, channels)] = map_ref[y]
    scored = scored_round(lax.axis_index("frame"), bits)
    for rnd, pay_ref in ((scored, pay_b_ref), (1 - scored, pay_a_ref)):
        write_payload(rnd, cells_ref, subs_ref, counts_ref, pay_ref, band_ref, band)


def payload_ids(pay_ref):
    chunks = pay_ref.shape[0] // (LANES + 4)
    ids = pay_ref[pl.ds(chunks * LANES, 4 * chunks), :].astype(jnp.float32)
    both = jnp.max(ids[2 * chunks :]) > 1.5
    return join_rows(ids[:chunks]), join_rows(ids[chunks : 2 * chunks]), both


def fold(tok_ref, fold_ref):
    half, width = fold_ref.shape[0], tok_ref.shape[1]
    fold_ref[:, pl.ds(0, width)] = tok_ref[pl.ds(0, half), :]
    fold_ref[:, pl.ds(width, width)] = tok_ref[pl.ds(half, half), :]


def pick(fold_ref, column):
    half, width = fold_ref.shape[0], fold_ref.shape[1] // 2
    upper = column >= half
    got = jnp.dot(
        one_hot(jnp.where(upper, column - half, column), half),
        fold_ref[...],
        preferred_element_type=jnp.float32,
    )
    return jnp.where(upper, got[:, width:], got[:, :width])


def band_kernel(cuts, map_ref, bands_ref):
    height, width, channels = map_ref.shape
    cut_y, cut_x = cuts
    band, span = height // cut_y, width // cut_x
    wide = span + 2 * MARGIN
    blank = jnp.zeros((wide, channels), jnp.float32)
    edge = jnp.zeros((MARGIN, channels), jnp.float32)
    for r in range(cut_y):
        slabs = [[] for _ in range(cut_x)]
        for yl in range(band + 2 * REACH):
            y = r * band - REACH + yl
            if 0 <= y < height:
                row = jnp.concatenate([edge, map_ref[y].astype(jnp.float32), edge], axis=0)
            for c in range(cut_x):
                slabs[c].append(row[c * span : c * span + wide] if 0 <= y < height else blank)
        for c in range(cut_x):
            bands_ref[:, pl.ds((r * cut_x + c) * channels, channels)] = jnp.concatenate(
                slabs[c], axis=0
            ).astype(jnp.bfloat16)


def lane_sums(rows):
    return jnp.concatenate(
        [
            jnp.sum(rows[i : i + LANES].T, axis=0, keepdims=True)
            for i in range(0, rows.shape[0], LANES)
        ],
        axis=1,
    )


def scores_of(tok_ref, rows):
    return lax.dot_general(tok_ref[...], rows, NT, preferred_element_type=jnp.float32)


def exp_sums(tok_ref, rows, scale):
    expo = jnp.exp2(scores_of(tok_ref, rows) * (scale * LOG2E))
    return jnp.sum(expo, axis=0, keepdims=True)


def safe_lse(tok_ref, rows, scale):
    scores = scores_of(tok_ref, rows) * scale
    top = jnp.max(scores, axis=0, keepdims=True)
    return top + jnp.log(jnp.sum(jnp.exp(scores - top), axis=0, keepdims=True))


def conf_kernel(
    bits, scale, counts_ref, cells_ref, list_ref, tok_ref, far_tok_ref, conf_ref,
    mine_ref, theirs_ref, own_fold, far_fold, score_ref, sums_ref,
):
    tok_count = tok_ref.shape[0]
    slots = cells_ref.shape[-1]
    scored = scored_round(lax.axis_index("frame"), bits)
    fold(tok_ref, own_fold)
    fold(far_tok_ref, far_fold)
    here, there = cells_ref[0, scored], list_ref[0:2, :]
    columns = [here[0:1], here[1:2], there[0:1], there[1:2]]
    here_own, here_far, there_own, there_far = to_columns(
        [split_rows(row.astype(jnp.float32)) for row in columns]
    )
    own_cell = jnp.concatenate([here_own, there_far], axis=0)
    far_cell = jnp.concatenate([here_far, there_own], axis=0)
    score_ref[...] = jnp.zeros_like(score_ref)
    sums_ref[...] = jnp.ones_like(sums_ref)

    def tiles(starts):
        mine = [pick(own_fold, own_cell[i : i + HALF]) for i in starts]
        theirs = [pick(far_fold, far_cell[i : i + HALF]) for i in starts]
        one = [exp_sums(far_tok_ref, rows.astype(jnp.bfloat16), scale) for rows in mine]
        two = [exp_sums(tok_ref, rows.astype(jnp.bfloat16), scale) for rows in theirs]
        for n, i in enumerate(starts):
            rows = pl.ds(i, HALF)
            mine_ref[rows, :] = mine[n].astype(jnp.bfloat16)
            theirs_ref[rows, :] = theirs[n].astype(jnp.bfloat16)
            score_ref[:, rows] = lane_sums(mine[n] * theirs[n])
            sums_ref[0:1, rows] = one[n]
            sums_ref[1:2, rows] = two[n]

    def safe(starts):
        for i in starts:
            rows = pl.ds(i, HALF)
            sums_ref[0:1, rows] = safe_lse(far_tok_ref, mine_ref[rows, :], scale)
            sums_ref[1:2, rows] = safe_lse(tok_ref, theirs_ref[rows, :], scale)

    counts = jnp.where(scored == 0, counts_ref[:, 0:1], counts_ref[:, 1:2])
    here_more = jnp.max(counts) > HALF
    there_more = jnp.max(list_ref[2:3, :]) > HALF
    first = [0, slots]
    here_rest = list(range(HALF, slots, HALF))
    there_rest = [i + slots for i in here_rest]
    tiles(first)
    pl.when(here_more)(functools.partial(tiles, here_rest))
    pl.when(there_more)(functools.partial(tiles, there_rest))
    least = jnp.min(sums_ref[...])
    most = jnp.max(sums_ref[...])
    sums_ref[...] = jnp.log(sums_ref[...])

    @pl.when(jnp.logical_not((least > 1e-30) & (most < 1e30)))
    def _():
        safe(first)
        pl.when(here_more)(functools.partial(safe, here_rest))
        pl.when(there_more)(functools.partial(safe, there_rest))

    conf = score_ref[...] * (2.0 * scale) + 2.0 * math.log(tok_count)
    conf = conf - (sums_ref[0:1, :] + sums_ref[1:2, :])
    conf_ref[0:1, :] = conf[:, :slots]
    conf_ref[1:3, :] = jnp.broadcast_to(conf[:, slots:], (2, slots))


def heat_kernel(cuts, band, span, pay_ref, bands_ref, conf_ref, out_ref):
    cut_y, cut_x = cuts
    slots = conf_ref.shape[1]
    channels = pay_ref.shape[1]
    high, wide = band + 2 * REACH, span + 2 * MARGIN
    far_y, far_x, both = payload_ids(pay_ref)
    at_y = jnp.floor((far_y + 0.5) * (1.0 / band))
    at_x = jnp.floor((far_x + 0.5) * (1.0 / span))
    local_y = far_y - at_y * band + REACH
    local_x = far_x - at_x * span + MARGIN
    which = jnp.broadcast_to(at_y * cut_x + at_x, (channels, slots)).astype(jnp.bfloat16)
    scale = channels**-0.5 * LOG2E
    out_ref[2:3, :] = conf_ref[2:3, :]

    def windows(i):
        query = jnp.concatenate(
            [pay_ref[pl.ds(n, LANES), :] for n in range(i, i + HALF, LANES)], axis=1
        )
        zero = jnp.zeros_like(query)
        right = jnp.concatenate(
            [jnp.where(which[:, i : i + HALF] == n, query, zero) for n in range(cut_y * cut_x)],
            axis=0,
        )
        heat = jnp.dot(bands_ref[...], right, preferred_element_type=jnp.float32)
        ly = local_y[:, i : i + HALF].astype(jnp.int32)
        lx = local_x[:, i : i + HALF].astype(jnp.int32)
        shift_x = lax.broadcasted_iota(jnp.int32, (8, HALF), 0) - lx + REACH & 7
        tile_x = lx + shift_x - REACH >> 3
        rows = []
        for yl in range(high):
            found = heat[yl * wide : yl * wide + 8]
            for t in range(1, wide // 8):
                start = yl * wide + 8 * t
                found = jnp.where(tile_x == t, heat[start : start + 8], found)
            rows.append(found)
        kept, deltas = [], []
        for n in range(8):
            shift_y = n - ly + REACH & 7
            tile_y = ly + shift_y - REACH >> 3
            found = rows[n]
            for t, other in enumerate(rows[n + 8 :: 8]):
                found = jnp.where(tile_y == t + 1, other, found)
            keep = (shift_x < SIDE) & (shift_y < SIDE)
            kept.append(jnp.where(keep, found, -jnp.inf))
            deltas.append((shift_y - REACH).astype(jnp.float32))
        top = jnp.max(functools.reduce(jnp.maximum, kept), axis=0, keepdims=True)
        expos = [jnp.exp2((one - top) * scale) for one in kept]
        total = sum(expos[1:], expos[0])
        total_y = sum(expo * delta for expo, delta in zip(expos, deltas))
        whole = jnp.sum(total, axis=0, keepdims=True)
        delta_x = (shift_x - REACH).astype(jnp.float32)
        out_ref[0:1, pl.ds(i, HALF)] = jnp.sum(total * delta_x, axis=0, keepdims=True) / whole
        out_ref[1:2, pl.ds(i, HALF)] = jnp.sum(total_y, axis=0, keepdims=True) / whole

    @pl.when(jnp.logical_not(both))
    def _():
        out_ref[0:2, :] = jnp.zeros((2, slots), jnp.float32)
        windows(0)

    @pl.when(both)
    def _():
        for i in range(0, slots, HALF):
            windows(i)


def early_kernel(bits, counts_ref, conf_ref, got_ref, conf_out, base_ref):
    scored = scored_round(lax.axis_index("frame"), bits)
    slots = conf_ref.shape[1]
    lane = lax.broadcasted_iota(jnp.int32, (1, slots), 1)
    for rnd in range(2):
        valid = lane < counts_ref[:, rnd : rnd + 1]
        mine = scored == rnd
        conf = jnp.where(mine, conf_ref[0:1, :], got_ref[2:3, :])
        conf_out[0, rnd : rnd + 1, :] = jnp.where(valid, conf, 0.0)
        offs = jnp.where(mine, 0.0, got_ref[0:2, :])
        base_ref[2 * rnd : 2 * rnd + 2, :] = jnp.where(valid, offs, 0.0)
        base_ref[4 + rnd : 5 + rnd, :] = jnp.where(valid & mine, 1.0, 0.0)


def late_kernel(base_ref, got_ref, offs_out):
    for rnd in range(2):
        valid = base_ref[4 + rnd : 5 + rnd, :] > 0.5
        base = base_ref[2 * rnd : 2 * rnd + 2, :]
        offs_out[0, rnd] = jnp.where(valid, got_ref[0:2, :], base)


def body(tokens, fine_map, matches, subcells, counts):
    frames = lax.axis_size("frame")
    top = frames.bit_length() - 1
    bits = [top - 1 - rnd for rnd in range(matches.shape[1])]
    slots = matches.shape[3]
    tok_count, width = tokens.shape
    height, fine_width, channels = fine_map.shape
    bands = math.gcd(height, 4)
    cuts = (math.gcd(height, 2), math.gcd(fine_width, 2))
    band, span = height // cuts[0], fine_width // cuts[1]
    cells = (band + 2 * REACH) * (span + 2 * MARGIN)
    tiles = cuts[0] * cuts[1]
    id_rows = 4 * slots // LANES
    f32, bf16 = jnp.float32, jnp.bfloat16

    sends = [(i, i ^ 1 << bits[1 - scored_round(i, bits)]) for i in range(frames)]
    backs = [(b, a) for a, b in sends]
    scale = 10.0 / width
    small = pltpu.CompilerParams(vmem_limit_bytes=24 << 20)

    def hint(flops, moved=0):
        return pl.CostEstimate(flops=flops, bytes_accessed=moved, transcendentals=0)

    far_tokens = lax.ppermute(tokens, "frame", sends)
    far_list = pl.pallas_call(
        functools.partial(list_kernel, bits),
        out_shape=jax.ShapeDtypeStruct((4, slots), jnp.int32),
        in_specs=[VMEM] * 2,
        out_specs=VMEM,
        name="scored_list",
        cost_estimate=hint(1 << 34),
        compiler_params=small,
    )(matches, counts)
    far_list = lax.ppermute(far_list, "frame", sends)
    payload = jax.ShapeDtypeStruct((slots + id_rows, channels), bf16)
    map_rows = pltpu.VMEM((height // bands * fine_width, bands * channels), bf16)
    pay_a, pay_b = pl.pallas_call(
        functools.partial(query_kernel, bits),
        out_shape=(payload, payload),
        in_specs=[VMEM] * 4,
        out_specs=(VMEM,) * 2,
        scratch_shapes=[map_rows],
        name="gather_queries",
        cost_estimate=hint(1 << 30),
        compiler_params=small,
    )(fine_map, matches, subcells, counts)
    pay_b = lax.ppermute(pay_b, "frame", backs)
    pay_a = lax.ppermute(pay_a, "frame", sends)
    band_map = pl.pallas_call(
        functools.partial(band_kernel, cuts),
        out_shape=jax.ShapeDtypeStruct((cells, tiles * channels), bf16),
        in_specs=[VMEM],
        out_specs=VMEM,
        name="bands",
        compiler_params=small,
    )(fine_map)

    conf = pl.pallas_call(
        functools.partial(conf_kernel, bits, scale),
        out_shape=jax.ShapeDtypeStruct((3, slots), f32),
        in_specs=[VMEM] * 5,
        out_specs=VMEM,
        scratch_shapes=[pltpu.VMEM((2 * slots, width), bf16)] * 2
        + [pltpu.VMEM((tok_count // 2, 2 * width), bf16)] * 2
        + [pltpu.VMEM((1, 2 * slots), f32), pltpu.VMEM((2, 2 * slots), f32)],
        name="confidences",
        cost_estimate=hint(1 << 34),
        compiler_params=small,
    )(counts, matches, far_list, tokens, far_tokens)

    def windows(pay, conf):
        return pl.pallas_call(
            functools.partial(heat_kernel, cuts, band, span),
            out_shape=jax.ShapeDtypeStruct((3, slots), f32),
            in_specs=[VMEM] * 3,
            out_specs=VMEM,
            name="window_offsets",
            cost_estimate=hint(1 << 33, 2 * cells * tiles * channels),
            compiler_params=small,
        )(pay, band_map, conf)

    answer_a = windows(pay_a, conf)
    got_a = lax.ppermute(answer_a, "frame", backs)
    answer_b = windows(pay_b, answer_a)
    got_b = lax.ppermute(answer_b, "frame", sends)

    rounds = len(bits)
    conf_out, base = pl.pallas_call(
        functools.partial(early_kernel, bits),
        out_shape=(
            jax.ShapeDtypeStruct((1, rounds, slots), f32),
            jax.ShapeDtypeStruct((3 * rounds, slots), f32),
        ),
        in_specs=[VMEM] * 3,
        out_specs=(VMEM,) * 2,
        name="early_outputs",
        compiler_params=small,
    )(counts, conf, got_a)
    offs_out = pl.pallas_call(
        late_kernel,
        out_shape=jax.ShapeDtypeStruct((1, rounds, 2, slots), f32),
        in_specs=[VMEM] * 2,
        out_specs=VMEM,
        name="late_outputs",
        compiler_params=small,
    )(base, got_b)
    return conf_out, offs_out


def solution(mesh):
    return jax.shard_map(
        body,
        mesh=mesh,
        in_specs=(
            P("frame", None),
            P("frame", None, None),
            P("frame", None, None, None),
            P("frame", None, None, None),
            P("frame", None),
        ),
        out_specs=(P("frame", None, None), P("frame", None, None, None)),
        check_vma=False,
    )
```

```python
import functools
import math

import jax
import jax.numpy as jnp
from jax import lax
from jax.experimental import pallas as pl
from jax.experimental.pallas import tpu as pltpu
from jax.sharding import PartitionSpec as P

LANES = 128
REACH = 2
SIDE = 2 * REACH + 1
MARGIN = 4
HALF = 256
LOG2E = math.log2(math.e)
VMEM = pl.BlockSpec(memory_space=pltpu.VMEM)
SMEM = pl.BlockSpec(memory_space=pltpu.SMEM)
HBM = pl.BlockSpec(memory_space=pltpu.HBM)
ANY = pl.BlockSpec(memory_space=pl.ANY)
NT = (((1,), (1,)), ((), ()))


def scored_round(frame, bits):
    return 1 ^ (frame >> bits[0] & 1) ^ (frame >> bits[1] & 1)


def split_rows(row):
    return jnp.concatenate(
        [row[:, i * LANES : (i + 1) * LANES] for i in range(row.shape[1] // LANES)], axis=0
    )


def join_rows(rows):
    return jnp.concatenate([rows[i : i + 1] for i in range(rows.shape[0])], axis=1)


def to_columns(rows):
    chunks = rows[0].shape[0]
    table = jnp.concatenate(rows, axis=0)
    spare = LANES - table.shape[0]
    table = jnp.concatenate([table, jnp.zeros((spare, LANES), jnp.float32)], axis=0).T
    return [
        jnp.concatenate(
            [table[:, n * chunks + i : n * chunks + i + 1] for i in range(chunks)], axis=0
        )
        for n in range(len(rows))
    ]


def one_hot(column, width):
    lanes = lax.broadcasted_iota(jnp.int32, (column.shape[0], width), 1).astype(jnp.float32)
    return jnp.where(lanes == column, 1.0, 0.0).astype(jnp.bfloat16)


def fine_point(cells, subs, coarse_width):
    return (
        2 * lax.div(cells, coarse_width) + lax.shift_right_logical(subs, 1),
        2 * lax.rem(cells, coarse_width) + jnp.bitwise_and(subs, 1),
    )


def write_payload(rnd, cells_ref, subs_ref, counts_ref, pay_ref, band_ref, band):
    slots = cells_ref.shape[-1]
    width = band_ref.shape[0] // band
    coarse_width = width // 2
    channels = pay_ref.shape[1]
    bands = band_ref.shape[1] // channels
    cells, subs = cells_ref[0, rnd], subs_ref[0, rnd]
    own, far = split_rows(cells[0:1]), split_rows(cells[1:2])
    own_y, own_x = fine_point(own, split_rows(subs[0:1]), coarse_width)
    far_y, far_x = fine_point(far, split_rows(subs[1:2]), coarse_width)
    count = jnp.where(rnd == 0, counts_ref[:, 0:1], counts_ref[:, 1:2])
    chunks = slots // LANES
    halves = jnp.broadcast_to(lax.div(count + (HALF - 1), HALF), (2 * chunks, LANES))
    pay_ref[pl.ds(slots, 4 * chunks), :] = (
        jnp.concatenate([far_y, far_x, halves], axis=0).astype(jnp.float32).astype(jnp.bfloat16)
    )
    rows = [own_x, lax.rem(own_y, band), lax.div(own_y, band)]
    x, in_band, which = to_columns([one.astype(jnp.float32) for one in rows])
    hot_x = one_hot(x, width)
    in_band = jnp.broadcast_to(in_band, hot_x.shape).astype(jnp.bfloat16)
    zero = jnp.zeros_like(hot_x)
    hot = jnp.concatenate([jnp.where(in_band == y, hot_x, zero) for y in range(band)], axis=1)
    got = jnp.dot(hot, band_ref[...], preferred_element_type=jnp.float32)
    query = jnp.zeros((slots, channels), jnp.float32)
    for r in range(bands):
        query = jnp.where(which == r, got[:, r * channels : (r + 1) * channels], query)
    for i in range(0, slots, LANES):
        pay_ref[pl.ds(i, LANES), :] = query[i : i + LANES].T.astype(jnp.bfloat16)


def list_kernel(bits, cells_ref, counts_ref, list_ref):
    rnd = 1 - scored_round(lax.axis_index("frame"), bits)
    count = jnp.where(rnd == 0, counts_ref[:, 0:1], counts_ref[:, 1:2])
    list_ref[0:2, :] = cells_ref[0, rnd]
    list_ref[2:4, :] = jnp.broadcast_to(count, (2, list_ref.shape[1]))


def query_kernel(
    bits, map_ref, cells_ref, subs_ref, counts_ref, pay_a_ref, pay_b_ref, band_ref
):
    height, width, channels = map_ref.shape
    bands = band_ref.shape[1] // channels
    band = height // bands
    for y in range(height):
        r, yl = divmod(y, band)
        band_ref[pl.ds(yl * width, width), pl.ds(r * channels, channels)] = map_ref[y]
    scored = scored_round(lax.axis_index("frame"), bits)
    for rnd, pay_ref in ((scored, pay_b_ref), (1 - scored, pay_a_ref)):
        write_payload(rnd, cells_ref, subs_ref, counts_ref, pay_ref, band_ref, band)


def payload_ids(pay_ref):
    chunks = pay_ref.shape[0] // (LANES + 4)
    ids = pay_ref[pl.ds(chunks * LANES, 4 * chunks), :].astype(jnp.float32)
    both = jnp.max(ids[2 * chunks :]) > 1.5
    return join_rows(ids[:chunks]), join_rows(ids[chunks : 2 * chunks]), both


def fold(tok_ref, fold_ref):
    half, width = fold_ref.shape[0], tok_ref.shape[1]
    fold_ref[:, pl.ds(0, width)] = tok_ref[pl.ds(0, half), :]
    fold_ref[:, pl.ds(width, width)] = tok_ref[pl.ds(half, half), :]


def pick(fold_ref, column):
    half, width = fold_ref.shape[0], fold_ref.shape[1] // 2
    upper = column >= half
    got = jnp.dot(
        one_hot(jnp.where(upper, column - half, column), half),
        fold_ref[...],
        preferred_element_type=jnp.float32,
    )
    return jnp.where(upper, got[:, width:], got[:, :width])


def band_kernel(cuts, map_ref, bands_ref):
    height, width, channels = map_ref.shape
    cut_y, cut_x = cuts
    band, span = height // cut_y, width // cut_x
    wide = span + 2 * MARGIN
    blank = jnp.zeros((wide, channels), jnp.float32)
    edge = jnp.zeros((MARGIN, channels), jnp.float32)
    for r in range(cut_y):
        slabs = [[] for _ in range(cut_x)]
        for yl in range(band + 2 * REACH):
            y = r * band - REACH + yl
            if 0 <= y < height:
                row = jnp.concatenate([edge, map_ref[y].astype(jnp.float32), edge], axis=0)
            for c in range(cut_x):
                slabs[c].append(row[c * span : c * span + wide] if 0 <= y < height else blank)
        for c in range(cut_x):
            bands_ref[:, pl.ds((r * cut_x + c) * channels, channels)] = jnp.concatenate(
                slabs[c], axis=0
            ).astype(jnp.bfloat16)


def lane_sums(rows):
    return jnp.concatenate(
        [
            jnp.sum(rows[i : i + LANES].T, axis=0, keepdims=True)
            for i in range(0, rows.shape[0], LANES)
        ],
        axis=1,
    )


def scores_of(tok_ref, rows):
    return lax.dot_general(tok_ref[...], rows, NT, preferred_element_type=jnp.float32)


def exp_sums(tok_ref, rows, scale):
    expo = jnp.exp2(scores_of(tok_ref, rows) * (scale * LOG2E))
    return jnp.sum(expo, axis=0, keepdims=True)


def safe_lse(tok_ref, rows, scale):
    scores = scores_of(tok_ref, rows) * scale
    top = jnp.max(scores, axis=0, keepdims=True)
    return top + jnp.log(jnp.sum(jnp.exp(scores - top), axis=0, keepdims=True))


def conf_kernel(
    bits, scale, counts_ref, cells_ref, list_ref, tok_ref, far_tok_ref, conf_ref,
    mine_ref, theirs_ref, own_fold, far_fold, score_ref, sums_ref,
):
    tok_count = tok_ref.shape[0]
    slots = cells_ref.shape[-1]
    scored = scored_round(lax.axis_index("frame"), bits)
    fold(tok_ref, own_fold)
    fold(far_tok_ref, far_fold)
    here, there = cells_ref[0, scored], list_ref[0:2, :]
    columns = [here[0:1], here[1:2], there[0:1], there[1:2]]
    here_own, here_far, there_own, there_far = to_columns(
        [split_rows(row.astype(jnp.float32)) for row in columns]
    )
    own_cell = jnp.concatenate([here_own, there_far], axis=0)
    far_cell = jnp.concatenate([here_far, there_own], axis=0)
    score_ref[...] = jnp.zeros_like(score_ref)
    sums_ref[...] = jnp.ones_like(sums_ref)

    def tiles(starts):
        mine = [pick(own_fold, own_cell[i : i + HALF]) for i in starts]
        theirs = [pick(far_fold, far_cell[i : i + HALF]) for i in starts]
        one = [exp_sums(far_tok_ref, rows.astype(jnp.bfloat16), scale) for rows in mine]
        two = [exp_sums(tok_ref, rows.astype(jnp.bfloat16), scale) for rows in theirs]
        for n, i in enumerate(starts):
            rows = pl.ds(i, HALF)
            mine_ref[rows, :] = mine[n].astype(jnp.bfloat16)
            theirs_ref[rows, :] = theirs[n].astype(jnp.bfloat16)
            score_ref[:, rows] = lane_sums(mine[n] * theirs[n])
            sums_ref[0:1, rows] = one[n]
            sums_ref[1:2, rows] = two[n]

    def safe(starts):
        for i in starts:
            rows = pl.ds(i, HALF)
            sums_ref[0:1, rows] = safe_lse(far_tok_ref, mine_ref[rows, :], scale)
            sums_ref[1:2, rows] = safe_lse(tok_ref, theirs_ref[rows, :], scale)

    counts = jnp.where(scored == 0, counts_ref[:, 0:1], counts_ref[:, 1:2])
    here_more = jnp.max(counts) > HALF
    there_more = jnp.max(list_ref[2:3, :]) > HALF
    first = [0, slots]
    here_rest = list(range(HALF, slots, HALF))
    there_rest = [i + slots for i in here_rest]
    tiles(first)
    pl.when(here_more)(functools.partial(tiles, here_rest))
    pl.when(there_more)(functools.partial(tiles, there_rest))
    least = jnp.min(sums_ref[...])
    most = jnp.max(sums_ref[...])
    sums_ref[...] = jnp.log(sums_ref[...])

    @pl.when(jnp.logical_not((least > 1e-30) & (most < 1e30)))
    def _():
        safe(first)
        pl.when(here_more)(functools.partial(safe, here_rest))
        pl.when(there_more)(functools.partial(safe, there_rest))

    conf = score_ref[...] * (2.0 * scale) + 2.0 * math.log(tok_count)
    conf = conf - (sums_ref[0:1, :] + sums_ref[1:2, :])
    conf_ref[0:1, :] = conf[:, :slots]
    conf_ref[1:3, :] = jnp.broadcast_to(conf[:, slots:], (2, slots))


def heat_kernel(cuts, band, span, pay_ref, bands_ref, conf_ref, out_ref):
    cut_y, cut_x = cuts
    slots = conf_ref.shape[1]
    channels = pay_ref.shape[1]
    high, wide = band + 2 * REACH, span + 2 * MARGIN
    far_y, far_x, both = payload_ids(pay_ref)
    at_y = jnp.floor((far_y + 0.5) * (1.0 / band))
    at_x = jnp.floor((far_x + 0.5) * (1.0 / span))
    local_y = far_y - at_y * band + REACH
    local_x = far_x - at_x * span + MARGIN
    which = jnp.broadcast_to(at_y * cut_x + at_x, (channels, slots)).astype(jnp.bfloat16)
    scale = channels**-0.5 * LOG2E
    if out_ref.shape[0] > 2:
        out_ref[2:3, :] = conf_ref[2:3, :]

    def windows(i):
        query = jnp.concatenate(
            [pay_ref[pl.ds(n, LANES), :] for n in range(i, i + HALF, LANES)], axis=1
        )
        zero = jnp.zeros_like(query)
        right = jnp.concatenate(
            [jnp.where(which[:, i : i + HALF] == n, query, zero) for n in range(cut_y * cut_x)],
            axis=0,
        )
        heat = jnp.dot(bands_ref[...], right, preferred_element_type=jnp.float32)
        ly = local_y[:, i : i + HALF].astype(jnp.int32)
        lx = local_x[:, i : i + HALF].astype(jnp.int32)
        shift_x = lax.broadcasted_iota(jnp.int32, (8, HALF), 0) - lx + REACH & 7
        tile_x = lx + shift_x - REACH >> 3
        rows = []
        for yl in range(high):
            found = heat[yl * wide : yl * wide + 8]
            for t in range(1, wide // 8):
                start = yl * wide + 8 * t
                found = jnp.where(tile_x == t, heat[start : start + 8], found)
            rows.append(found)
        kept, deltas = [], []
        for n in range(8):
            shift_y = n - ly + REACH & 7
            tile_y = ly + shift_y - REACH >> 3
            found = rows[n]
            for t, other in enumerate(rows[n + 8 :: 8]):
                found = jnp.where(tile_y == t + 1, other, found)
            keep = (shift_x < SIDE) & (shift_y < SIDE)
            kept.append(jnp.where(keep, found, -jnp.inf))
            deltas.append((shift_y - REACH).astype(jnp.float32))
        top = jnp.max(functools.reduce(jnp.maximum, kept), axis=0, keepdims=True)
        expos = [jnp.exp2((one - top) * scale) for one in kept]
        total = sum(expos[1:], expos[0])
        total_y = sum(expo * delta for expo, delta in zip(expos, deltas))
        whole = jnp.sum(total, axis=0, keepdims=True)
        delta_x = (shift_x - REACH).astype(jnp.float32)
        out_ref[0:1, pl.ds(i, HALF)] = jnp.sum(total * delta_x, axis=0, keepdims=True) / whole
        out_ref[1:2, pl.ds(i, HALF)] = jnp.sum(total_y, axis=0, keepdims=True) / whole

    @pl.when(jnp.logical_not(both))
    def _():
        out_ref[0:2, :] = jnp.zeros((2, slots), jnp.float32)
        windows(0)

    @pl.when(both)
    def _():
        for i in range(0, slots, HALF):
            windows(i)


def early_kernel(bits, counts_ref, conf_ref, got_ref, conf_out, base_ref):
    scored = scored_round(lax.axis_index("frame"), bits)
    slots = conf_ref.shape[1]
    lane = lax.broadcasted_iota(jnp.int32, (1, slots), 1)
    for rnd in range(2):
        valid = lane < counts_ref[:, rnd : rnd + 1]
        mine = scored == rnd
        conf = jnp.where(mine, conf_ref[0:1, :], got_ref[2:3, :])
        conf_out[0, rnd : rnd + 1, :] = jnp.where(valid, conf, 0.0)
        offs = jnp.where(mine, 0.0, got_ref[0:2, :])
        base_ref[2 * rnd : 2 * rnd + 2, :] = jnp.where(valid, offs, 0.0)
        base_ref[4 + rnd : 5 + rnd, :] = jnp.where(valid & mine, 1.0, 0.0)


def late_kernel(base_ref, got_ref, offs_out):
    for rnd in range(2):
        valid = base_ref[4 + rnd : 5 + rnd, :] > 0.5
        base = base_ref[2 * rnd : 2 * rnd + 2, :]
        offs_out[0, rnd] = jnp.where(valid, got_ref[0:2, :], base)


def body(tokens, fine_map, matches, subcells, counts):
    frames = lax.axis_size("frame")
    top = frames.bit_length() - 1
    bits = [top - 1 - rnd for rnd in range(matches.shape[1])]
    slots = matches.shape[3]
    tok_count, width = tokens.shape
    height, fine_width, channels = fine_map.shape
    bands = math.gcd(height, 4)
    cuts = (math.gcd(height, 2), math.gcd(fine_width, 2))
    band, span = height // cuts[0], fine_width // cuts[1]
    cells = (band + 2 * REACH) * (span + 2 * MARGIN)
    tiles = cuts[0] * cuts[1]
    id_rows = 4 * slots // LANES
    f32, bf16 = jnp.float32, jnp.bfloat16

    sends = [(i, i ^ 1 << bits[1 - scored_round(i, bits)]) for i in range(frames)]
    backs = [(b, a) for a, b in sends]
    scale = 10.0 / width
    small = pltpu.CompilerParams(vmem_limit_bytes=24 << 20)

    def hint(flops, moved=0):
        return pl.CostEstimate(flops=flops, bytes_accessed=moved, transcendentals=0)

    far_tokens = lax.ppermute(tokens, "frame", sends)
    far_list = pl.pallas_call(
        functools.partial(list_kernel, bits),
        out_shape=jax.ShapeDtypeStruct((4, slots), jnp.int32),
        in_specs=[VMEM] * 2,
        out_specs=VMEM,
        name="scored_list",
        cost_estimate=hint(1 << 34),
        compiler_params=small,
    )(matches, counts)
    far_list = lax.ppermute(far_list, "frame", sends)
    payload = jax.ShapeDtypeStruct((slots + id_rows, channels), bf16)
    map_rows = pltpu.VMEM((height // bands * fine_width, bands * channels), bf16)
    pay_a, pay_b = pl.pallas_call(
        functools.partial(query_kernel, bits),
        out_shape=(payload, payload),
        in_specs=[VMEM] * 4,
        out_specs=(VMEM,) * 2,
        scratch_shapes=[map_rows],
        name="gather_queries",
        cost_estimate=hint(1 << 30),
        compiler_params=small,
    )(fine_map, matches, subcells, counts)
    pay_b = lax.ppermute(pay_b, "frame", backs)
    pay_a = lax.ppermute(pay_a, "frame", sends)
    band_map = pl.pallas_call(
        functools.partial(band_kernel, cuts),
        out_shape=jax.ShapeDtypeStruct((cells, tiles * channels), bf16),
        in_specs=[VMEM],
        out_specs=VMEM,
        name="bands",
        compiler_params=small,
    )(fine_map)

    conf = pl.pallas_call(
        functools.partial(conf_kernel, bits, scale),
        out_shape=jax.ShapeDtypeStruct((3, slots), f32),
        in_specs=[VMEM] * 5,
        out_specs=VMEM,
        scratch_shapes=[pltpu.VMEM((2 * slots, width), bf16)] * 2
        + [pltpu.VMEM((tok_count // 2, 2 * width), bf16)] * 2
        + [pltpu.VMEM((1, 2 * slots), f32), pltpu.VMEM((2, 2 * slots), f32)],
        name="confidences",
        cost_estimate=hint(1 << 34),
        compiler_params=small,
    )(counts, matches, far_list, tokens, far_tokens)

    def windows(pay, conf, rows):
        return pl.pallas_call(
            functools.partial(heat_kernel, cuts, band, span),
            out_shape=jax.ShapeDtypeStruct((rows, slots), f32),
            in_specs=[VMEM] * 3,
            out_specs=VMEM,
            name="window_offsets",
            cost_estimate=hint(1 << 33, 2 * cells * tiles * channels),
            compiler_params=small,
        )(pay, band_map, conf)

    answer_a = windows(pay_a, conf, 3)
    got_a = lax.ppermute(answer_a, "frame", backs)
    answer_b = windows(pay_b, answer_a, 2)
    got_b = lax.ppermute(answer_b, "frame", sends)

    rounds = len(bits)
    conf_out, base = pl.pallas_call(
        functools.partial(early_kernel, bits),
        out_shape=(
            jax.ShapeDtypeStruct((1, rounds, slots), f32),
            jax.ShapeDtypeStruct((3 * rounds, slots), f32),
        ),
        in_specs=[VMEM] * 3,
        out_specs=(VMEM,) * 2,
        name="early_outputs",
        compiler_params=small,
    )(counts, conf, got_a)
    offs_out = pl.pallas_call(
        late_kernel,
        out_shape=jax.ShapeDtypeStruct((1, rounds, 2, slots), f32),
        in_specs=[VMEM] * 2,
        out_specs=VMEM,
        name="late_outputs",
        compiler_params=small,
    )(base, got_b)
    return conf_out, offs_out


def solution(mesh):
    return jax.shard_map(
        body,
        mesh=mesh,
        in_specs=(
            P("frame", None),
            P("frame", None, None),
            P("frame", None, None, None),
            P("frame", None, None, None),
            P("frame", None),
        ),
        out_specs=(P("frame", None, None), P("frame", None, None, None)),
        check_vma=False,
    )
```
